32 devices in a mesh: sample: 8 (over y, x, core), slab: 4 (over z).
Axes of the slice: x: 2, y: 2, z: 4, core: 2. Of those that a mesh axis runs over, the one named last changes fastest.
Arguments:
- volume: bfloat16 [4, 8, 16, 4096], P(None, 'sample', 'slab'), may hold values from -6 to 6
- cotangent: bfloat16 [128, 8, 4, 256], P(None, 'sample', 'slab'), may hold values from -1.25 to 1.25
- w_first: bfloat16 [27, 4, 32], replicated, may hold values from -0.625 to 0.625
- b_first: float32 [32], replicated, may hold values from -3 to 3
- w_second: bfloat16 [27, 32, 64], replicated, may hold values from -0.21875 to 0.21875
- b_second: float32 [64], replicated, may hold values from -3 to 3
- w_third: bfloat16 [27, 64, 128], replicated, may hold values from -0.15625 to 0.15625
- b_third: float32 [128], replicated, may hold values from -3 to 3
Outputs:
- features: bfloat16 [128, 8, 4, 256], P(None, 'sample', 'slab')
- kernel_grad_first: float32 [27, 4, 32], replicated
- bias_grad_first: float32 [32], replicated
- kernel_grad_second: float32 [27, 32, 64], replicated
- bias_grad_second: float32 [64], replicated
- kernel_grad_third: float32 [27, 64, 128], replicated
- bias_grad_third: float32 [128], replicated
The draws below stay inside these ranges and needn't reach their ends.
All inputs are finite; a program needn't handle non-finite values.
Results may differ from the reference program's by a relative error of at most 0.02.
Values may be sent and summed in bfloat16 or wider, within the bound.
A program may use at most 128 MiB of HBM per device.

```python
import jax
import jax.numpy as jnp
from jax import lax

C0 = 4
C1 = 32
C2 = 64
C3 = 128
SX = 32
SY = 128
BATCH = 8
NZ = 16


def steps_of(stream_key, extent, pieces, low, high):
    level, own = 1.0, jax.random.fold_in(stream_key, 6)
    for dim, blocks in pieces:
        steps = jnp.exp(jax.random.uniform(jax.random.fold_in(own, dim), (blocks,), jnp.float32, low / len(pieces), high / len(pieces)))
        level = level * jnp.repeat(steps, extent[dim] // blocks).reshape([-1 if axis == dim else 1 for axis in range(len(extent))])
    return level


def bell_draw(stream_key, dims, width, most, pieces=(), kind=jnp.bfloat16):
    entries = jax.random.normal(stream_key, dims, jnp.float32) * width
    if len(pieces) > 0:
        entries = steps_of(stream_key, dims, pieces, -0.22, 0.18) * entries
    return jnp.clip(entries, min=-most, max=most).astype(kind)


def setup_inputs(seed: int = 0) -> dict:
    arg_keys = jax.random.split(jax.random.key(seed), 9)
    volume = bell_draw(arg_keys[0], (C0, BATCH, NZ, SY * SX), 1.0, 6.0, ((1, 8), (2, 4)))
    cotangent = bell_draw(arg_keys[1], (C3, BATCH, NZ // 4, SY * SX // 16), (8.0 / (BATCH * NZ * SX * SY // 64) ** 0.5), 1.25, ((1, 8), (2, 4)))
    w_first = bell_draw(arg_keys[2], (27, C0, C1), (27 * C0) ** -0.5, 0.625)
    b_first = bell_draw(arg_keys[3], (C1,), 0.5, 3.0, (), jnp.float32)
    w_second = bell_draw(arg_keys[4], (27, C1, C2), (27 * C1) ** -0.5, 0.21875)
    b_second = bell_draw(arg_keys[5], (C2,), 0.5, 3.0, (), jnp.float32)
    w_third = bell_draw(arg_keys[6], (27, C2, C3), (27 * C2) ** -0.5, 0.15625)
    b_third = bell_draw(arg_keys[7], (C3,), 0.5, 3.0, (), jnp.float32)
    return dict(volume=volume, cotangent=cotangent, w_first=w_first, b_first=b_first, w_second=w_second, b_second=b_second, w_third=w_third, b_third=b_third)


def silu_slope(values):
    sigmoid = jax.nn.sigmoid(values)
    return sigmoid * (1.0 + values * (1.0 - sigmoid))


def shifted_views(source):
    padded = jnp.pad(source, ((0, 0), (1, 1), (1, 1), (1, 1)))
    depth_len, row_count, row_width = source.shape[1], source.shape[2], source.shape[3]
    shifted = []
    for tap_index in range(27):
        depth_start = tap_index // 9
        row_start = tap_index // 3 % 3
        column_start = tap_index % 3
        shifted.append(padded[:, depth_start:depth_start + depth_len, row_start:row_start + row_count, column_start:column_start + row_width])
    return shifted


def convolve(source, weight):
    summed = jnp.zeros((weight.shape[2],) + source.shape[1:], jnp.float32)
    for tap_index, shifted in enumerate(shifted_views(source)):
        summed = summed + jnp.einsum('izyx,io->ozyx', shifted.astype(jnp.float32), weight[tap_index].astype(jnp.float32))
    return summed


def weight_sums(source, delta_values):
    grads = delta_values.astype(jnp.float32)
    return jnp.stack([jnp.einsum('izyx,ozyx->io', shifted.astype(jnp.float32), grads) for shifted in shifted_views(source)])


def pool_cells(values):
    channels, depth_len, row_count, row_width = values.shape
    grouped = values.reshape(channels, depth_len // 2, 2, row_count // 2, 2, row_width // 2, 2)
    return grouped.mean(axis=(2, 4, 6))


def spread_cells(values):
    widened = jnp.repeat(jnp.repeat(jnp.repeat(values, 2, axis=1), 2, axis=2), 2, axis=3)
    return widened * 0.125


def reference(volume, cotangent, w_first, b_first, w_second, b_second, w_third, b_third):
    flipped_second = jnp.flip(w_second, 0).transpose(0, 2, 1)
    flipped_third = jnp.flip(w_third, 0).transpose(0, 2, 1)

    def per_sample(totals, sample):
        source = lax.dynamic_index_in_dim(volume, sample, 1, keepdims=False).reshape(C0, NZ, SY, SX)
        upstream = lax.dynamic_index_in_dim(cotangent, sample, 1, keepdims=False).reshape(C3, NZ // 4, SY // 4, SX // 4)
        first_pre = (convolve(source, w_first) + b_first[:, None, None, None]).astype(jnp.bfloat16)
        first_pooled = pool_cells(jax.nn.silu(first_pre.astype(jnp.float32))).astype(jnp.bfloat16)
        second_pre = (convolve(first_pooled, w_second) + b_second[:, None, None, None]).astype(jnp.bfloat16)
        second_pooled = pool_cells(jax.nn.silu(second_pre.astype(jnp.float32))).astype(jnp.bfloat16)
        third_pre = (convolve(second_pooled, w_third) + b_third[:, None, None, None]).astype(jnp.bfloat16)
        features = jax.nn.silu(third_pre.astype(jnp.float32)).astype(jnp.bfloat16)
        third_delta = (upstream.astype(jnp.float32) * silu_slope(third_pre.astype(jnp.float32))).astype(jnp.bfloat16)
        second_back = convolve(third_delta, flipped_third).astype(jnp.bfloat16)
        second_delta = (spread_cells(second_back.astype(jnp.float32)) * silu_slope(second_pre.astype(jnp.float32))).astype(jnp.bfloat16)
        first_back = convolve(second_delta, flipped_second).astype(jnp.bfloat16)
        first_delta = (spread_cells(first_back.astype(jnp.float32)) * silu_slope(first_pre.astype(jnp.float32))).astype(jnp.bfloat16)
        contribution = (
            weight_sums(source, first_delta),
            jnp.sum(first_delta.astype(jnp.float32), axis=(1, 2, 3)),
            weight_sums(first_pooled, second_delta),
            jnp.sum(second_delta.astype(jnp.float32), axis=(1, 2, 3)),
            weight_sums(second_pooled, third_delta),
            jnp.sum(third_delta.astype(jnp.float32), axis=(1, 2, 3)),
        )
        totals = jax.tree.map(jnp.add, totals, contribution)
        return totals, features.reshape(C3, NZ // 4, SY * SX // 16)

    initial = (
        jnp.zeros((27, C0, C1), jnp.float32),
        jnp.zeros((C1,), jnp.float32),
        jnp.zeros((27, C1, C2), jnp.float32),
        jnp.zeros((C2,), jnp.float32),
        jnp.zeros((27, C2, C3), jnp.float32),
        jnp.zeros((C3,), jnp.float32),
    )
    totals, stacked = lax.scan(per_sample, initial, jnp.arange(BATCH, dtype=jnp.int32))
    features = jnp.transpose(stacked, (1, 0, 2, 3))
    return (features, totals[0], totals[1], totals[2], totals[3], totals[4], totals[5])
```

```python
import functools

import jax
import jax.numpy as jnp
import numpy as np
from jax import lax
from jax.experimental import pallas as pl
from jax.experimental.pallas import tpu as pltpu
from jax.sharding import PartitionSpec as P

SY, SX = 32, 8
CELLS = SY * SX
F32, BF16 = jnp.float32, jnp.bfloat16
NT = (((1,), (1,)), ((), ()))
PLANE = 144
ROW_B3, ROW_G2, ROW_B2, ROW_G1, ROW_B1, ROWS = 1728, 1744, 2176, 2192, 2320, 2352


def selection():
    sel = np.zeros((PLANE, 288), np.float32)
    for y in range(6):
        for x in range(6):
            sy, y4 = divmod(y - 1, 4)
            sx, x4 = divmod(x - 1, 4)
            if sy < 0:
                base = (sx + 1) * 16 + x4 * 4
            elif sy == 0:
                base = 48 + (sx + 1) * 64 + y4 * 16 + x4 * 4
            else:
                base = 240 + (sx + 1) * 16 + x4 * 4
            for c in range(4):
                sel[(y * 6 + x) * 4 + c, base + c] = 1.0
    return sel


def dot(a, b):
    return jnp.dot(a, b, preferred_element_type=F32)


def dot_nt(a, b):
    return lax.dot_general(a, b, NT, preferred_element_type=F32)


def shifter():
    lane = lax.broadcasted_iota(jnp.int32, (1, CELLS), 1)
    row, column = lane // SX, lane % SX

    def shift(values, sy, sx):
        if sy == 0 and sx == 0:
            return values
        moved = pltpu.roll(values, (-(sy * SX + sx)) % CELLS, 1)
        keep = None
        for coordinate, size, step in ((row, SY, sy), (column, SX, sx)):
            if step != 0:
                inside = coordinate > 0 if step < 0 else coordinate < size - 1
                keep = inside if keep is None else keep & inside
        return jnp.where(keep, moved, 0.0)

    return shift


def activation(values):
    sigmoid = 1.0 / (1.0 + jnp.exp(-values))
    return values * sigmoid, sigmoid * (1.0 + values * (1.0 - sigmoid))


PHASES = [(a, b) for a in range(2) for b in range(2)]
TAPS = [(i, j, k) for i in range(3) for j in range(3) for k in range(3)]


def network_kernel(
    slabs, v_ref, cot_ref, sel_ref, w1_ref, b1_ref, w2_ref, b2_ref, w3_ref, b3_ref, w2f_ref,
    w3f_ref, feat_ref, pack_ref, rv, rf, rs, rd3, rd2, f1, f2, d3, d2, stack, a1, w1b, slope1,
    p2, slope2, s3, s3d, p2d, send_sem, recv_sem,
):
    me = lax.axis_index("slab")
    has_prev, has_next = me > 0, me < slabs - 1
    shift = shifter()

    barrier = pltpu.get_barrier_semaphore()
    for there, peer in ((has_prev, me - 1), (has_next, me + 1)):

        @pl.when(there)
        def _():
            pl.semaphore_signal(
                barrier, inc=1, device_id={"slab": peer}, device_id_type=pl.DeviceIdType.MESH
            )

    @pl.when(has_prev & has_next)
    def _():
        pl.semaphore_wait(barrier, 2)

    @pl.when(~(has_prev & has_next))
    def _():
        pl.semaphore_wait(barrier, 1)

    def copies(index, up_src, down_src, landing):
        up = pltpu.make_async_remote_copy(
            src_ref=up_src, dst_ref=landing.at[0], send_sem=send_sem.at[index, 0],
            recv_sem=recv_sem.at[index, 0], device_id={"slab": me + 1},
            device_id_type=pl.DeviceIdType.MESH,
        )
        down = pltpu.make_async_remote_copy(
            src_ref=down_src, dst_ref=landing.at[1], send_sem=send_sem.at[index, 1],
            recv_sem=recv_sem.at[index, 1], device_id={"slab": me - 1},
            device_id_type=pl.DeviceIdType.MESH,
        )
        return up, down

    def start(pair):
        @pl.when(has_next)
        def _():
            pair[0].start()

        @pl.when(has_prev)
        def _():
            pair[1].start()

    def arrive(pair, landing):
        @pl.when(has_prev)
        def _():
            pair[0].wait_recv()

        @pl.when(me == 0)
        def _():
            landing[0] = jnp.zeros(landing.shape[1:], landing.dtype)

        @pl.when(has_next)
        def _():
            pair[1].wait_recv()

        @pl.when(me == slabs - 1)
        def _():
            landing[1] = jnp.zeros(landing.shape[1:], landing.dtype)

    halo_v = copies(0, v_ref.at[3], v_ref.at[0], rv)
    start(halo_v)
    w1_wide = w1_ref[...]
    for index in range(16):
        (qy, qx), (py, px) = PHASES[index // 4], PHASES[index % 4]
        offset = ((2 * qy + py) * 6 + 2 * qx + px) * 4
        wide = w1_wide if offset == 0 else pltpu.roll(w1_wide, offset, 1)
        w1b[index * 32 : (index + 1) * 32, :] = wide.astype(BF16)
    bias_one = jnp.concatenate([b1_ref[...]] * 16, axis=0)
    a1[6 * PLANE :, :] = jnp.zeros((a1.shape[0] - 6 * PLANE, CELLS), BF16)

    def build_plane(z, plane):
        values = plane.astype(F32)
        row = 0
        for sy, lo, hi in ((-1, 48, 64), (0, 0, 64), (1, 0, 16)):
            for sx in (-1, 0, 1):
                stack[row : row + hi - lo, :] = shift(values[lo:hi], sy, sx).astype(BF16)
                row += hi - lo
        a1[z * PLANE : (z + 1) * PLANE, :] = dot(sel_ref[...], stack[...]).astype(BF16)

    def first_layer(z):
        pre = dot(w1b[:, : 3 * PLANE], a1[z * PLANE : (z + 3) * PLANE, :]) + bias_one
        active, slope = activation(pre.astype(BF16).astype(F32))
        slope1[z] = slope * 0.125
        parts = []
        for q in range(4):
            block = active[q * 128 : (q + 1) * 128]
            parts.append(block[0:32] + block[32:64] + block[64:96] + block[96:128])
        return parts

    for z in range(4):
        build_plane(z + 1, v_ref[z])
    part1, part2 = first_layer(1), first_layer(2)
    arrive(halo_v, rv)
    build_plane(0, rv[0])
    build_plane(5, rv[1])
    part0, part3 = first_layer(0), first_layer(3)
    for q in range(4):
        f1[0, q * 32 : (q + 1) * 32, :] = ((part0[q] + part1[q]) * 0.125).astype(BF16)
        f1[1, q * 32 : (q + 1) * 32, :] = ((part2[q] + part3[q]) * 0.125).astype(BF16)

    halo_f = copies(1, f1.at[1], f1.at[0], rf)
    start(halo_f)

    def spread_block(target, block, channels, place, flipped):
        for tap_index, (i, j, k) in enumerate(TAPS):
            steps = (2 - i, 2 - j, 2 - k) if flipped else (i, j, k)
            phase = [position - step for position, step in zip(place, steps)]
            if all(0 <= value <= 1 for value in phase):
                lane = (phase[0] * 4 + phase[1] * 2 + phase[2]) * CELLS
                target[
                    tap_index * channels : (tap_index + 1) * channels, lane : lane + CELLS
                ] = block

    def place_plane(target, take, channels, z, flipped):
        for y in range(4):
            sy, qy = divmod(y - 1, 2)
            for x in range(4):
                sx, qx = divmod(x - 1, 2)
                block = take(qy * 2 + qx)
                if sy != 0 or sx != 0:
                    block = shift(block.astype(F32), sy, sx).astype(BF16)
                spread_block(target, block, channels, (z, y, x), flipped)

    for z in range(2):
        place_plane(p2, lambda q: f1[z, q * 32 : (q + 1) * 32, :], 32, z + 1, False)
    arrive(halo_f, rf)
    for side, z in ((0, 0), (1, 3)):
        place_plane(p2, lambda q: rf[side, q * 32 : (q + 1) * 32, :], 32, z, False)
    pooled = jnp.zeros((64, CELLS), F32)
    for half in range(2):
        lanes = slice(half * 1024, (half + 1) * 1024)
        pre = dot(w2_ref[...], p2[:, lanes]) + b2_ref[...]
        active, slope = activation(pre.astype(BF16).astype(F32))
        slope2[:, lanes] = slope * 0.125
        for q in range(4):
            pooled = pooled + active[:, q * CELLS : (q + 1) * CELLS]
    f2[...] = (pooled * 0.125).astype(BF16)

    halo_s = copies(2, f2, f2, rs)
    start(halo_s)

    def place_coarse(target, plane, channels, i, flipped):
        values = plane.astype(F32)
        for j in range(3):
            for k in range(3):
                sy, sx = (1 - j, 1 - k) if flipped else (j - 1, k - 1)
                row = ((i * 3 + j) * 3 + k) * channels
                target[row : row + channels, :] = shift(values, sy, sx).astype(BF16)

    place_coarse(s3, f2[...], 64, 1, False)
    arrive(halo_s, rs)
    place_coarse(s3, rs[0], 64, 0, False)
    place_coarse(s3, rs[1], 64, 2, False)
    pre = dot(w3_ref[...], s3[...]) + b3_ref[...]
    active, slope = activation(pre.astype(BF16).astype(F32))
    feat_ref[...] = active.astype(BF16)
    d3[...] = (cot_ref[...].astype(F32) * slope).astype(BF16)

    halo_d3 = copies(3, d3, d3, rd3)
    start(halo_d3)
    pack_ref[0:ROW_B3, :] = dot_nt(s3[...], d3[...]).astype(BF16)
    pack_ref[ROW_B3:ROW_G2, :] = dot_nt(jnp.ones((16, CELLS), BF16), d3[...]).astype(BF16)
    place_coarse(s3d, d3[...], 128, 1, True)
    arrive(halo_d3, rd3)
    place_coarse(s3d, rd3[1], 128, 0, True)
    place_coarse(s3d, rd3[0], 128, 2, True)
    back = dot(w3f_ref[...], s3d[...]).astype(BF16).astype(F32)
    for p in range(8):
        d2[p // 4, :, p % 4 * CELLS : (p % 4 + 1) * CELLS] = (
            back * slope2[:, p * CELLS : (p + 1) * CELLS]
        ).astype(BF16)

    halo_d2 = copies(4, d2.at[1], d2.at[0], rd2)
    start(halo_d2)
    grad2 = dot_nt(p2[:, :1024], d2[0]) + dot_nt(p2[:, 1024:], d2[1])
    pack_ref[ROW_G2:ROW_B2, :] = jnp.concatenate([grad2[:432], grad2[432:]], axis=1).astype(BF16)
    ones = jnp.ones((16, 1024), BF16)
    sum2 = dot_nt(ones, d2[0]) + dot_nt(ones, d2[1])
    pack_ref[ROW_B2:ROW_G1, :] = jnp.concatenate([sum2, sum2], axis=1).astype(BF16)
    for z in range(2):
        place_plane(
            p2d, lambda q: d2[z, :, q * CELLS : (q + 1) * CELLS], 64, z + 1, True
        )
    arrive(halo_d2, rd2)
    for side, z in ((0, 0), (1, 3)):
        place_plane(
            p2d, lambda q: rd2[side, :, q * CELLS : (q + 1) * CELLS], 64, z, True
        )
    first_back = dot(w2f_ref[...], p2d[...]).astype(BF16).astype(F32)
    grad1 = jnp.zeros((512, 512), F32)
    sum1 = jnp.zeros((32, CELLS), F32)
    for z in range(4):
        blocks = []
        for index in range(16):
            lane = ((z // 2) * 4 + index // 4) * CELLS
            delta = (
                first_back[:, lane : lane + CELLS] * slope1[z, index * 32 : (index + 1) * 32, :]
            ).astype(BF16)
            sum1 = sum1 + delta.astype(F32)
            blocks.append(delta)
        delta = jnp.concatenate(blocks, axis=0)
        grad1 = grad1 + dot_nt(delta, a1[z * PLANE : z * PLANE + 512, :])
    folded = jnp.zeros((32, 512), F32)
    for index in range(16):
        (qy, qx), (py, px) = PHASES[index // 4], PHASES[index % 4]
        offset = ((2 * qy + py) * 6 + 2 * qx + px) * 4
        rows = grad1[index * 32 : (index + 1) * 32]
        folded = folded + (rows if offset == 0 else pltpu.roll(rows, 512 - offset, 1))
    for q in range(4):
        pack_ref[ROW_G1 + q * 32 : ROW_G1 + (q + 1) * 32, :] = folded[
            :, q * 128 : (q + 1) * 128
        ].astype(BF16)
    total = jnp.sum(sum1, axis=1, keepdims=True)
    pack_ref[ROW_B1:ROWS, :] = jnp.broadcast_to(total, (32, 128)).astype(BF16)
    pack_ref[ROWS:, :] = jnp.zeros((pack_ref.shape[0] - ROWS, 128), BF16)

    for pair in (halo_v, halo_f, halo_s, halo_d3, halo_d2):

        @pl.when(has_next)
        def _():
            pair[0].wait_send()

        @pl.when(has_prev)
        def _():
            pair[1].wait_send()


def sum_kernel(
    samples, slabs, pack_ref, out_ref, land_a, land_b, part, whole, send_a, recv_a, send_b,
    recv_b, send_c, recv_c, send_d, recv_d,
):
    s, z = lax.axis_index("sample"), lax.axis_index("slab")
    chunk = pack_ref.shape[0] // samples
    piece = chunk // slabs
    mesh_id = pl.DeviceIdType.MESH
    sample_peers = [lax.rem(s + k, samples) for k in range(1, samples)]
    slab_peers = [lax.rem(z + k, slabs) for k in range(1, slabs)]

    barrier = pltpu.get_barrier_semaphore()
    for axis, peers in (("sample", sample_peers), ("slab", slab_peers)):
        for peer in peers:
            pl.semaphore_signal(barrier, inc=1, device_id={axis: peer}, device_id_type=mesh_id)
    pl.semaphore_wait(barrier, samples + slabs - 2)

    def rows(start, size):
        return pl.ds(pl.multiple_of(start, 16), size)

    def exchange(axis, peers, mine, source, target, arrival, send, recv):
        for peer in peers:
            pltpu.make_async_remote_copy(
                src_ref=source(peer), dst_ref=target, send_sem=send.at[peer],
                recv_sem=recv.at[mine], device_id={axis: peer}, device_id_type=mesh_id,
            ).start()

        def settle(peer):
            pltpu.make_async_remote_copy(
                src_ref=source(peer), dst_ref=arrival(peer), send_sem=send.at[peer],
                recv_sem=recv.at[peer], device_id={axis: peer}, device_id_type=mesh_id,
            ).wait()

        return settle

    settle = exchange(
        "sample", sample_peers, s, lambda peer: pack_ref.at[rows(peer * chunk, chunk)],
        land_a.at[s], lambda peer: land_a.at[peer], send_a, recv_a,
    )
    total = pack_ref[rows(s * chunk, chunk), :].astype(F32)
    for peer in sample_peers:
        settle(peer)
        total = total + land_a[peer].astype(F32)
    part[...] = total.astype(BF16)

    settle = exchange(
        "slab", slab_peers, z, lambda peer: part.at[rows(peer * piece, piece)],
        land_b.at[z], lambda peer: land_b.at[peer], send_b, recv_b,
    )
    total = part[rows(z * piece, piece), :].astype(F32)
    for peer in slab_peers:
        settle(peer)
        total = total + land_b[peer].astype(F32)
    own = rows(s * chunk + z * piece, piece)
    whole[own, :] = total.astype(BF16)

    settle = exchange(
        "slab", slab_peers, z, lambda peer: whole.at[own], whole.at[own],
        lambda peer: whole.at[rows(s * chunk + peer * piece, piece)], send_c, recv_c,
    )
    for peer in slab_peers:
        settle(peer)
    band = rows(s * chunk, chunk)
    settle = exchange(
        "sample", sample_peers, s, lambda peer: whole.at[band], whole.at[band],
        lambda peer: whole.at[rows(peer * chunk, chunk)], send_d, recv_d,
    )
    out_ref[band, :] = whole[band, :].astype(F32)
    for peer in sample_peers:
        settle(peer)
        out_ref[rows(peer * chunk, chunk), :] = whole[rows(peer * chunk, chunk), :].astype(F32)


def per_device(volume, cotangent, w_first, b_first, w_second, b_second, w_third, b_third):
    samples, slabs = lax.axis_size("sample"), lax.axis_size("slab")
    unit = 16 * samples * slabs
    pack_rows = -(-ROWS // unit) * unit
    vmem = pl.BlockSpec(memory_space=pltpu.VMEM)

    phased = volume.reshape(4, 4, SY, 4, SX, 4).transpose(1, 3, 5, 0, 2, 4).reshape(4, 64, CELLS)
    w1 = jnp.pad(
        w_first.astype(F32).reshape(3, 3, 3, 4, 32), ((0, 0), (0, 3), (0, 3), (0, 0), (0, 0))
    )
    w1 = jnp.pad(w1.reshape(3 * PLANE, 32).T, ((0, 0), (0, 512 - 3 * PLANE)))
    w2 = w_second.reshape(27 * 32, 64).T
    w3 = w_third.reshape(27 * 64, 128).T
    w2f = w_second.transpose(1, 0, 2).reshape(32, 27 * 64)
    w3f = w_third.transpose(1, 0, 2).reshape(64, 27 * 128)

    features, pack = pl.pallas_call(
        functools.partial(network_kernel, slabs),
        out_shape=(
            jax.ShapeDtypeStruct((128, CELLS), BF16),
            jax.ShapeDtypeStruct((pack_rows, 128), BF16),
        ),
        in_specs=[vmem] * 11,
        out_specs=(vmem, vmem),
        scratch_shapes=[
            pltpu.VMEM((2, 64, CELLS), BF16),
            pltpu.VMEM((2, 128, CELLS), BF16),
            pltpu.VMEM((2, 64, CELLS), BF16),
            pltpu.VMEM((2, 128, CELLS), BF16),
            pltpu.VMEM((2, 64, 4 * CELLS), BF16),
            pltpu.VMEM((2, 128, CELLS), BF16),
            pltpu.VMEM((64, CELLS), BF16),
            pltpu.VMEM((128, CELLS), BF16),
            pltpu.VMEM((2, 64, 4 * CELLS), BF16),
            pltpu.VMEM((288, CELLS), BF16),
            pltpu.VMEM((944, CELLS), BF16),
            pltpu.VMEM((512, 512), BF16),
            pltpu.VMEM((4, 512, CELLS), F32),
            pltpu.VMEM((864, 8 * CELLS), BF16),
            pltpu.VMEM((64, 8 * CELLS), F32),
            pltpu.VMEM((1728, CELLS), BF16),
            pltpu.VMEM((3456, CELLS), BF16),
            pltpu.VMEM((1728, 8 * CELLS), BF16),
            pltpu.SemaphoreType.DMA((5, 2)),
            pltpu.SemaphoreType.DMA((5, 2)),
        ],
        compiler_params=pltpu.CompilerParams(
            collective_id=0, has_side_effects=True, vmem_limit_bytes=48 * 2**20
        ),
        name="network",
    )(
        phased, cotangent.reshape(128, CELLS), jnp.asarray(selection(), BF16), w1,
        b_first[:, None], w2, b_second[:, None], w3, b_third[:, None], w2f, w3f,
    )

    chunk = pack_rows // samples
    summed = pl.pallas_call(
        functools.partial(sum_kernel, samples, slabs),
        out_shape=jax.ShapeDtypeStruct((pack_rows, 128), F32),
        in_specs=[vmem],
        out_specs=vmem,
        scratch_shapes=[
            pltpu.VMEM((samples, chunk, 128), BF16),
            pltpu.VMEM((slabs, chunk // slabs, 128), BF16),
            pltpu.VMEM((chunk, 128), BF16),
            pltpu.VMEM((pack_rows, 128), BF16),
        ]
        + [pltpu.SemaphoreType.DMA((n,)) for n in (samples, samples, slabs, slabs) * 1]
        + [pltpu.SemaphoreType.DMA((n,)) for n in (slabs, slabs, samples, samples)],
        compiler_params=pltpu.CompilerParams(
            collective_id=1, has_side_effects=True, vmem_limit_bytes=32 * 2**20
        ),
        name="sum_all",
    )(pack)

    kernel_third = summed[:ROW_B3].reshape(27, 64, 128)
    bias_third = summed[ROW_B3]
    grad2 = summed[ROW_G2:ROW_B2]
    kernel_second = jnp.concatenate([grad2[:, :64], grad2[:, 64:]], axis=0).reshape(27, 32, 64)
    bias_second = summed[ROW_B2, :64]
    grad1 = summed[ROW_G1:ROW_B1].reshape(4, 32, 128).transpose(1, 0, 2).reshape(32, 512)
    grad1 = grad1[:, : 3 * PLANE].reshape(32, 3, 6, 6, 4)[:, :, :3, :3, :]
    kernel_first = grad1.transpose(1, 2, 3, 4, 0).reshape(27, 4, 32)
    bias_first = summed[ROW_B1:ROWS, 0]
    return (
        features.reshape(128, 1, 1, CELLS),
        kernel_first,
        bias_first,
        kernel_second,
        bias_second,
        kernel_third,
        bias_third,
    )


def solution(mesh):
    split = P(None, "sample", "slab", None)
    in_specs = (split, split, P(), P(), P(), P(), P(), P())
    out_specs = (split, P(), P(), P(), P(), P(), P())
    return jax.shard_map(
        per_device, mesh=mesh, in_specs=in_specs, out_specs=out_specs, check_vma=False
    )
```

```python
import functools

import jax
import jax.numpy as jnp
import numpy as np
from jax import lax
from jax.experimental import pallas as pl
from jax.experimental.pallas import tpu as pltpu
from jax.sharding import PartitionSpec as P

SY, SX = 32, 8
CELLS = SY * SX
F32, BF16 = jnp.float32, jnp.bfloat16
NT = (((1,), (1,)), ((), ()))
PLANE = 144
ROW_B3, ROW_G2, ROW_B2, ROW_G1, ROW_B1, ROWS = 1728, 1744, 2176, 2192, 2320, 2352


def selection():
    sel = np.zeros((PLANE, 288), np.float32)
    for y in range(6):
        for x in range(6):
            sy, y4 = divmod(y - 1, 4)
            sx, x4 = divmod(x - 1, 4)
            if sy < 0:
                base = (sx + 1) * 16 + x4 * 4
            elif sy == 0:
                base = 48 + (sx + 1) * 64 + y4 * 16 + x4 * 4
            else:
                base = 240 + (sx + 1) * 16 + x4 * 4
            for c in range(4):
                sel[(y * 6 + x) * 4 + c, base + c] = 1.0
    return sel


def phase_spread():
    out = np.zeros((128, 16, SY, SX), np.float32)
    for y in range(4):
        for x in range(4):
            for column in range(SX):
                out[y * 4 * SX + column * 4 + x, y * 4 + x, :, column] = 1.0
    return out.reshape(128, 16 * CELLS)


def plane_order():
    out = np.zeros((256, 256), np.float32)
    for phase in range(16):
        for c in range(4):
            for z in range(4):
                out[z * 64 + phase * 4 + c, phase * 16 + c * 4 + z] = 1.0
    return out


def dot(a, b):
    return jnp.dot(a, b, preferred_element_type=F32)


def dot_nt(a, b):
    return lax.dot_general(a, b, NT, preferred_element_type=F32)


def shifter():
    lane = lax.broadcasted_iota(jnp.int32, (1, CELLS), 1)
    row, column = lane // SX, lane % SX

    def shift(values, sy, sx):
        if sy == 0 and sx == 0:
            return values
        moved = pltpu.roll(values, (-(sy * SX + sx)) % CELLS, 1)
        keep = None
        for coordinate, size, step in ((row, SY, sy), (column, SX, sx)):
            if step != 0:
                inside = coordinate > 0 if step < 0 else coordinate < size - 1
                keep = inside if keep is None else keep & inside
        return jnp.where(keep, moved, 0.0)

    return shift


def activation(values):
    sigmoid = 1.0 / (1.0 + jnp.exp(-values))
    return values * sigmoid, sigmoid * (1.0 + values * (1.0 - sigmoid))


PHASES = [(a, b) for a in range(2) for b in range(2)]
TAPS = [(i, j, k) for i in range(3) for j in range(3) for k in range(3)]


def network_kernel(
    slabs, vol_ref, cot_ref, sel_ref, spread_ref, order_ref, w1_ref, b1_ref, w2_ref, b2_ref, w3_ref, b3_ref, w2f_ref,
    w3f_ref, feat_ref, pack_ref, v_ref, rows_ref, rv, rf, rs, rd3, rd2, f1, f2, d3, d2, stack, a1, w1b, slope1,
    p2, slope2, s3, s3d, p2d, send_sem, recv_sem,
):
    me = lax.axis_index("slab")
    has_prev, has_next = me > 0, me < slabs - 1
    shift = shifter()

    barrier = pltpu.get_barrier_semaphore()
    for there, peer in ((has_prev, me - 1), (has_next, me + 1)):

        @pl.when(there)
        def _():
            pl.semaphore_signal(
                barrier, inc=1, device_id={"slab": peer}, device_id_type=pl.DeviceIdType.MESH
            )

    @pl.when(has_prev & has_next)
    def _():
        pl.semaphore_wait(barrier, 2)

    @pl.when(~(has_prev & has_next))
    def _():
        pl.semaphore_wait(barrier, 1)

    def copies(index, up_src, down_src, landing):
        up = pltpu.make_async_remote_copy(
            src_ref=up_src, dst_ref=landing.at[0], send_sem=send_sem.at[index, 0],
            recv_sem=recv_sem.at[index, 0], device_id={"slab": me + 1},
            device_id_type=pl.DeviceIdType.MESH,
        )
        down = pltpu.make_async_remote_copy(
            src_ref=down_src, dst_ref=landing.at[1], send_sem=send_sem.at[index, 1],
            recv_sem=recv_sem.at[index, 1], device_id={"slab": me - 1},
            device_id_type=pl.DeviceIdType.MESH,
        )
        return up, down

    def start(pair):
        @pl.when(has_next)
        def _():
            pair[0].start()

        @pl.when(has_prev)
        def _():
            pair[1].start()

    def arrive(pair, landing):
        @pl.when(has_prev)
        def _():
            pair[0].wait_recv()

        @pl.when(me == 0)
        def _():
            landing[0] = jnp.zeros(landing.shape[1:], landing.dtype)

        @pl.when(has_next)
        def _():
            pair[1].wait_recv()

        @pl.when(me == slabs - 1)
        def _():
            landing[1] = jnp.zeros(landing.shape[1:], landing.dtype)

    for row in range(SY):
        rows_ref[row * 16 : (row + 1) * 16, :] = vol_ref[:, row * 128 : (row + 1) * 128]
    own_row = lax.broadcasted_iota(jnp.int32, (1, CELLS), 1) // SX
    phases = []
    for phase in range(16):
        spread = dot(rows_ref[...], spread_ref[:, phase * CELLS : (phase + 1) * CELLS])
        picked = spread[0:16]
        for row in range(1, SY):
            picked = jnp.where(own_row == row, spread[row * 16 : (row + 1) * 16], picked)
        phases.append(picked.astype(BF16))
    ordered = dot(order_ref[...], jnp.concatenate(phases, axis=0)).astype(BF16)
    for z in range(4):
        v_ref[z] = ordered[z * 64 : (z + 1) * 64]
    halo_v = copies(0, v_ref.at[3], v_ref.at[0], rv)
    start(halo_v)
    w1_wide = w1_ref[...]
    for index in range(16):
        (qy, qx), (py, px) = PHASES[index // 4], PHASES[index % 4]
        offset = ((2 * qy + py) * 6 + 2 * qx + px) * 4
        wide = w1_wide if offset == 0 else pltpu.roll(w1_wide, offset, 1)
        w1b[index * 32 : (index + 1) * 32, :] = wide.astype(BF16)
    bias_one = jnp.concatenate([b1_ref[...]] * 16, axis=0)
    a1[6 * PLANE :, :] = jnp.zeros((a1.shape[0] - 6 * PLANE, CELLS), BF16)

    def build_plane(z, plane):
        values = plane.astype(F32)
        row = 0
        for sy, lo, hi in ((-1, 48, 64), (0, 0, 64), (1, 0, 16)):
            for sx in (-1, 0, 1):
                stack[row : row + hi - lo, :] = shift(values[lo:hi], sy, sx).astype(BF16)
                row += hi - lo
        a1[z * PLANE : (z + 1) * PLANE, :] = dot(sel_ref[...], stack[...]).astype(BF16)

    def first_layer(z):
        pre = dot(w1b[:, : 3 * PLANE], a1[z * PLANE : (z + 3) * PLANE, :]) + bias_one
        active, slope = activation(pre.astype(BF16).astype(F32))
        slope1[z] = slope * 0.125
        parts = []
        for q in range(4):
            block = active[q * 128 : (q + 1) * 128]
            parts.append(block[0:32] + block[32:64] + block[64:96] + block[96:128])
        return parts

    for z in range(4):
        build_plane(z + 1, v_ref[z])
    part1, part2 = first_layer(1), first_layer(2)
    arrive(halo_v, rv)
    build_plane(0, rv[0])
    build_plane(5, rv[1])
    part0, part3 = first_layer(0), first_layer(3)
    for q in range(4):
        f1[0, q * 32 : (q + 1) * 32, :] = ((part0[q] + part1[q]) * 0.125).astype(BF16)
        f1[1, q * 32 : (q + 1) * 32, :] = ((part2[q] + part3[q]) * 0.125).astype(BF16)

    halo_f = copies(1, f1.at[1], f1.at[0], rf)
    start(halo_f)

    def spread_block(target, block, channels, place, flipped):
        for tap_index, (i, j, k) in enumerate(TAPS):
            steps = (2 - i, 2 - j, 2 - k) if flipped else (i, j, k)
            phase = [position - step for position, step in zip(place, steps)]
            if all(0 <= value <= 1 for value in phase):
                lane = (phase[0] * 4 + phase[1] * 2 + phase[2]) * CELLS
                target[
                    tap_index * channels : (tap_index + 1) * channels, lane : lane + CELLS
                ] = block

    def place_plane(target, take, channels, z, flipped):
        for y in range(4):
            sy, qy = divmod(y - 1, 2)
            for x in range(4):
                sx, qx = divmod(x - 1, 2)
                block = take(qy * 2 + qx)
                if sy != 0 or sx != 0:
                    block = shift(block.astype(F32), sy, sx).astype(BF16)
                spread_block(target, block, channels, (z, y, x), flipped)

    for z in range(2):
        place_plane(p2, lambda q: f1[z, q * 32 : (q + 1) * 32, :], 32, z + 1, False)
    arrive(halo_f, rf)
    for side, z in ((0, 0), (1, 3)):
        place_plane(p2, lambda q: rf[side, q * 32 : (q + 1) * 32, :], 32, z, False)
    pooled = jnp.zeros((64, CELLS), F32)
    for half in range(2):
        lanes = slice(half * 1024, (half + 1) * 1024)
        pre = dot(w2_ref[...], p2[:, lanes]) + b2_ref[...]
        active, slope = activation(pre.astype(BF16).astype(F32))
        slope2[:, lanes] = slope * 0.125
        for q in range(4):
            pooled = pooled + active[:, q * CELLS : (q + 1) * CELLS]
    f2[...] = (pooled * 0.125).astype(BF16)

    halo_s = copies(2, f2, f2, rs)
    start(halo_s)

    def place_coarse(target, plane, channels, i, flipped):
        values = plane.astype(F32)
        for j in range(3):
            for k in range(3):
                sy, sx = (1 - j, 1 - k) if flipped else (j - 1, k - 1)
                row = ((i * 3 + j) * 3 + k) * channels
                target[row : row + channels, :] = shift(values, sy, sx).astype(BF16)

    place_coarse(s3, f2[...], 64, 1, False)
    arrive(halo_s, rs)
    place_coarse(s3, rs[0], 64, 0, False)
    place_coarse(s3, rs[1], 64, 2, False)
    pre = dot(w3_ref[...], s3[...]) + b3_ref[...]
    active, slope = activation(pre.astype(BF16).astype(F32))
    feat_ref[...] = active.astype(BF16)
    d3[...] = (cot_ref[...].astype(F32) * slope).astype(BF16)

    halo_d3 = copies(3, d3, d3, rd3)
    start(halo_d3)
    pack_ref[0:ROW_B3, :] = dot_nt(s3[...], d3[...]).astype(BF16)
    pack_ref[ROW_B3:ROW_G2, :] = dot_nt(jnp.ones((16, CELLS), BF16), d3[...]).astype(BF16)
    place_coarse(s3d, d3[...], 128, 1, True)
    arrive(halo_d3, rd3)
    place_coarse(s3d, rd3[1], 128, 0, True)
    place_coarse(s3d, rd3[0], 128, 2, True)
    back = dot(w3f_ref[...], s3d[...]).astype(BF16).astype(F32)
    for p in range(8):
        d2[p // 4, :, p % 4 * CELLS : (p % 4 + 1) * CELLS] = (
            back * slope2[:, p * CELLS : (p + 1) * CELLS]
        ).astype(BF16)

    halo_d2 = copies(4, d2.at[1], d2.at[0], rd2)
    start(halo_d2)
    grad2 = dot_nt(p2[:, :1024], d2[0]) + dot_nt(p2[:, 1024:], d2[1])
    pack_ref[ROW_G2:ROW_B2, :] = jnp.concatenate([grad2[:432], grad2[432:]], axis=1).astype(BF16)
    ones = jnp.ones((16, 1024), BF16)
    sum2 = dot_nt(ones, d2[0]) + dot_nt(ones, d2[1])
    pack_ref[ROW_B2:ROW_G1, :] = jnp.concatenate([sum2, sum2], axis=1).astype(BF16)
    for z in range(2):
        place_plane(
            p2d, lambda q: d2[z, :, q * CELLS : (q + 1) * CELLS], 64, z + 1, True
        )
    arrive(halo_d2, rd2)
    for side, z in ((0, 0), (1, 3)):
        place_plane(
            p2d, lambda q: rd2[side, :, q * CELLS : (q + 1) * CELLS], 64, z, True
        )
    first_back = dot(w2f_ref[...], p2d[...]).astype(BF16).astype(F32)
    grad1 = jnp.zeros((512, 512), F32)
    sum1 = jnp.zeros((32, CELLS), F32)
    for z in range(4):
        blocks = []
        for index in range(16):
            lane = ((z // 2) * 4 + index // 4) * CELLS
            delta = (
                first_back[:, lane : lane + CELLS] * slope1[z, index * 32 : (index + 1) * 32, :]
            ).astype(BF16)
            sum1 = sum1 + delta.astype(F32)
            blocks.append(delta)
        delta = jnp.concatenate(blocks, axis=0)
        grad1 = grad1 + dot_nt(delta, a1[z * PLANE : z * PLANE + 512, :])
    folded = jnp.zeros((32, 512), F32)
    for index in range(16):
        (qy, qx), (py, px) = PHASES[index // 4], PHASES[index % 4]
        offset = ((2 * qy + py) * 6 + 2 * qx + px) * 4
        rows = grad1[index * 32 : (index + 1) * 32]
        folded = folded + (rows if offset == 0 else pltpu.roll(rows, 512 - offset, 1))
    for q in range(4):
        pack_ref[ROW_G1 + q * 32 : ROW_G1 + (q + 1) * 32, :] = folded[
            :, q * 128 : (q + 1) * 128
        ].astype(BF16)
    total = jnp.sum(sum1, axis=1, keepdims=True)
    pack_ref[ROW_B1:ROWS, :] = jnp.broadcast_to(total, (32, 128)).astype(BF16)
    pack_ref[ROWS:, :] = jnp.zeros((pack_ref.shape[0] - ROWS, 128), BF16)

    for pair in (halo_v, halo_f, halo_s, halo_d3, halo_d2):

        @pl.when(has_next)
        def _():
            pair[0].wait_send()

        @pl.when(has_prev)
        def _():
            pair[1].wait_send()


def sum_kernel(
    samples, slabs, pack_ref, k1_ref, b1_ref, k2_ref, b2_ref, k3_ref, b3_ref, land_a, land_b, part, whole, turned, send_a, recv_a, send_b,
    recv_b, send_c, recv_c, send_d, recv_d,
):
    s, z = lax.axis_index("sample"), lax.axis_index("slab")
    chunk = pack_ref.shape[0] // samples
    piece = chunk // slabs
    mesh_id = pl.DeviceIdType.MESH
    sample_peers = [lax.rem(s + k, samples) for k in range(1, samples)]
    slab_peers = [lax.rem(z + k, slabs) for k in range(1, slabs)]

    barrier = pltpu.get_barrier_semaphore()
    for axis, peers in (("sample", sample_peers), ("slab", slab_peers)):
        for peer in peers:
            pl.semaphore_signal(barrier, inc=1, device_id={axis: peer}, device_id_type=mesh_id)
    pl.semaphore_wait(barrier, samples + slabs - 2)

    def rows(start, size):
        return pl.ds(pl.multiple_of(start, 16), size)

    def exchange(axis, peers, mine, source, target, arrival, send, recv):
        for peer in peers:
            pltpu.make_async_remote_copy(
                src_ref=source(peer), dst_ref=target, send_sem=send.at[peer],
                recv_sem=recv.at[mine], device_id={axis: peer}, device_id_type=mesh_id,
            ).start()

        def settle(peer):
            pltpu.make_async_remote_copy(
                src_ref=source(peer), dst_ref=arrival(peer), send_sem=send.at[peer],
                recv_sem=recv.at[peer], device_id={axis: peer}, device_id_type=mesh_id,
            ).wait()

        return settle

    settle = exchange(
        "sample", sample_peers, s, lambda peer: pack_ref.at[rows(peer * chunk, chunk)],
        land_a.at[s], lambda peer: land_a.at[peer], send_a, recv_a,
    )
    total = pack_ref[rows(s * chunk, chunk), :].astype(F32)
    for peer in sample_peers:
        settle(peer)
        total = total + land_a[peer].astype(F32)
    part[...] = total.astype(BF16)

    settle = exchange(
        "slab", slab_peers, z, lambda peer: part.at[rows(peer * piece, piece)],
        land_b.at[z], lambda peer: land_b.at[peer], send_b, recv_b,
    )
    total = part[rows(z * piece, piece), :].astype(F32)
    for peer in slab_peers:
        settle(peer)
        total = total + land_b[peer].astype(F32)
    own = rows(s * chunk + z * piece, piece)
    whole[own, :] = total.astype(BF16)

    settle = exchange(
        "slab", slab_peers, z, lambda peer: whole.at[own], whole.at[own],
        lambda peer: whole.at[rows(s * chunk + peer * piece, piece)], send_c, recv_c,
    )
    for peer in slab_peers:
        settle(peer)
    band = rows(s * chunk, chunk)
    settle = exchange(
        "sample", sample_peers, s, lambda peer: whole.at[band], whole.at[band],
        lambda peer: whole.at[rows(peer * chunk, chunk)], send_d, recv_d,
    )
    for peer in sample_peers:
        settle(peer)
    k3_ref[...] = whole[0:ROW_B3, :].astype(F32)
    b3_ref[...] = whole[ROW_B3:ROW_G2, :].astype(F32)[0:1]
    grad2 = whole[ROW_G2:ROW_B2, :].astype(F32)
    k2_ref[0:432, :] = grad2[:, :64]
    k2_ref[432:864, :] = grad2[:, 64:]
    b2_ref[...] = whole[ROW_B2:ROW_G1, :].astype(F32)[0:1, :64]
    for i in range(4):
        block = whole[ROW_G1 + i * 32 : ROW_G1 + (i + 1) * 32, :].astype(F32)
        turned[i * 128 : (i + 1) * 128, :] = block.T
    for i in range(3):
        for j in range(3):
            row = i * PLANE + j * 24
            k1_ref[(i * 3 + j) * 12 : (i * 3 + j + 1) * 12, :] = turned[row : row + 12, :]
    b1_ref[...] = whole[ROW_B1:ROWS, :].astype(F32).T[0:1, :]


def per_device(volume, cotangent, w_first, b_first, w_second, b_second, w_third, b_third):
    samples, slabs = lax.axis_size("sample"), lax.axis_size("slab")
    unit = 16 * samples * slabs
    pack_rows = -(-ROWS // unit) * unit
    vmem = pl.BlockSpec(memory_space=pltpu.VMEM)

    w1 = jnp.pad(
        w_first.astype(F32).reshape(3, 3, 3, 4, 32), ((0, 0), (0, 3), (0, 3), (0, 0), (0, 0))
    )
    w1 = jnp.pad(w1.reshape(3 * PLANE, 32).T, ((0, 0), (0, 512 - 3 * PLANE)))
    w2 = w_second.reshape(27 * 32, 64).T
    w3 = w_third.reshape(27 * 64, 128).T
    w2f = w_second.transpose(1, 0, 2).reshape(32, 27 * 64)
    w3f = w_third.transpose(1, 0, 2).reshape(64, 27 * 128)

    features, pack = pl.pallas_call(
        functools.partial(network_kernel, slabs),
        out_shape=(
            jax.ShapeDtypeStruct((128, CELLS), BF16),
            jax.ShapeDtypeStruct((pack_rows, 128), BF16),
        ),
        in_specs=[vmem] * 13,
        out_specs=(vmem, vmem),
        scratch_shapes=[
            pltpu.VMEM((4, 64, CELLS), BF16),
            pltpu.VMEM((512, 128), BF16),
            pltpu.VMEM((2, 64, CELLS), BF16),
            pltpu.VMEM((2, 128, CELLS), BF16),
            pltpu.VMEM((2, 64, CELLS), BF16),
            pltpu.VMEM((2, 128, CELLS), BF16),
            pltpu.VMEM((2, 64, 4 * CELLS), BF16),
            pltpu.VMEM((2, 128, CELLS), BF16),
            pltpu.VMEM((64, CELLS), BF16),
            pltpu.VMEM((128, CELLS), BF16),
            pltpu.VMEM((2, 64, 4 * CELLS), BF16),
            pltpu.VMEM((288, CELLS), BF16),
            pltpu.VMEM((944, CELLS), BF16),
            pltpu.VMEM((512, 512), BF16),
            pltpu.VMEM((4, 512, CELLS), F32),
            pltpu.VMEM((864, 8 * CELLS), BF16),
            pltpu.VMEM((64, 8 * CELLS), F32),
            pltpu.VMEM((1728, CELLS), BF16),
            pltpu.VMEM((3456, CELLS), BF16),
            pltpu.VMEM((1728, 8 * CELLS), BF16),
            pltpu.SemaphoreType.DMA((5, 2)),
            pltpu.SemaphoreType.DMA((5, 2)),
        ],
        compiler_params=pltpu.CompilerParams(
            collective_id=0, has_side_effects=True, vmem_limit_bytes=48 * 2**20
        ),
        name="network",
    )(
        volume.reshape(16, 16 * CELLS), cotangent.reshape(128, CELLS),
        jnp.asarray(selection(), BF16), jnp.asarray(phase_spread(), BF16),
        jnp.asarray(plane_order(), BF16), w1,
        b_first[:, None], w2, b_second[:, None], w3, b_third[:, None], w2f, w3f,
    )

    chunk = pack_rows // samples
    k1, b1, k2, b2, k3, b3 = pl.pallas_call(
        functools.partial(sum_kernel, samples, slabs),
        out_shape=tuple(
            jax.ShapeDtypeStruct(shape, F32)
            for shape in ((108, 32), (1, 32), (864, 64), (1, 64), (1728, 128), (1, 128))
        ),
        in_specs=[vmem],
        out_specs=(vmem,) * 6,
        scratch_shapes=[
            pltpu.VMEM((samples, chunk, 128), BF16),
            pltpu.VMEM((slabs, chunk // slabs, 128), BF16),
            pltpu.VMEM((chunk, 128), BF16),
            pltpu.VMEM((pack_rows, 128), BF16),
            pltpu.VMEM((512, 32), F32),
        ]
        + [pltpu.SemaphoreType.DMA((n,)) for n in (samples, samples, slabs, slabs)]
        + [pltpu.SemaphoreType.DMA((n,)) for n in (slabs, slabs, samples, samples)],
        compiler_params=pltpu.CompilerParams(
            collective_id=1, has_side_effects=True, vmem_limit_bytes=32 * 2**20
        ),
        name="sum_all",
    )(pack)

    return (
        features.reshape(128, 1, 1, CELLS),
        k1.reshape(27, 4, 32),
        b1.reshape(32),
        k2.reshape(27, 32, 64),
        b2.reshape(64),
        k3.reshape(27, 64, 128),
        b3.reshape(128),
    )


def solution(mesh):
    split = P(None, "sample", "slab", None)
    in_specs = (split, split, P(), P(), P(), P(), P(), P())
    out_specs = (split, P(), P(), P(), P(), P(), P())
    return jax.shard_map(
        per_device, mesh=mesh, in_specs=in_specs, out_specs=out_specs, check_vma=False
    )
```
